32 devices in a mesh: groups: 2 (over x), pair: 4 (over y, core), day: 4 (over z).
Axes of the slice: x: 2, y: 2, z: 4, core: 2. Of those that a mesh axis runs over, the one named last changes fastest.
Arguments:
- spectra: bfloat16 [8, 512, 4, 2048], P(('groups', 'day'), 'pair'), parts along dimension 0, may hold values from -6 to 6
- sub_pick: int32 [4, 2], P('day'), may hold values from 0 to 3, as said below
- pair_list: int32 [4, 2, 2], P('pair'), may hold values from 0 to 3, as said below
- slot_count: int32 [4], P('pair'), may hold values from 1 to 2
Outputs:
- stacks: float32 [16, 128, 8192], P(('groups', 'pair'), 'day'), parts along dimension 0
The draws below stay inside these ranges and needn't reach their ends.
There are 2 independent parts, one for each index of `groups`. The reference program is written for one: setup_inputs(seed, part) draws one part's arguments, and reference() takes and returns one part's arrays. A program takes and returns all parts, laid end to end along the dimension named above; an argument that names none is the same for every part. Nothing has to cross between parts.
Inputs may be any that keep to these rules, and one draw needn't show every extreme that they name: `sub_pick`: in each row the 2 values are distinct. `pair_list`: for owner p every slot has a <= b <= a + 3 and p - 3 <= a, b <= p + 3.
All inputs are finite; a program needn't handle non-finite values.
Results may differ from the reference program's by a relative error of at most 0.0037.
Values may be sent and summed in bfloat16 or wider, within the bound.
A program may use at most 128 MiB of HBM per device.

```python
import jax
import jax.numpy as jnp
from jax import lax

CH_BLK = 128
F = 1024
LAGS = 64
SUBS = 4
SUB = 2
P_DEV = 2
REACH = 3
OFFS = 4
N_DAY_WIN = 4
CHANNELS = 512
SLOTS = 8
N_PAIR = 4


def draw_sub_pick(key, part):
    key = jax.random.fold_in(key, 5)
    first, second = jax.random.split(key)
    scores = jax.random.randint(first, (N_DAY_WIN, SUBS), 0, 1 << 20) * SUBS + jnp.arange(SUBS, dtype=jnp.int32)[None, :]
    order = jnp.argsort(scores, axis=1)[:, :SUB].astype(jnp.int32)
    forced = jnp.concatenate([jnp.array([SUBS - 1], jnp.int32), jnp.arange(SUB - 1, dtype=jnp.int32)])
    chosen = jax.random.randint(second, (), 0, N_DAY_WIN)
    rows = jnp.arange(N_DAY_WIN)[:, None]
    return jnp.where(rows == chosen, forced[None, :], order).astype(jnp.int32)


def draw_pair_list(key, part):
    key = jax.random.fold_in(key, 11)
    first, second = jax.random.split(key)
    owner = jnp.arange(N_PAIR, dtype=jnp.int32)[:, None]
    column = jnp.arange(P_DEV, dtype=jnp.int32)[None, :]
    offsets = jax.random.randint(first, (N_PAIR, P_DEV), 0, OFFS)
    lower = jax.random.randint(second, (N_PAIR, P_DEV), 0, 2 * REACH + 1)
    start = owner - REACH + lower % (2 * REACH - offsets + 1)
    start = jnp.where(column == 0, owner - REACH, start)
    start = jnp.where(column == 1, owner + REACH - offsets, start)
    start = jnp.clip(start, 0, N_PAIR - 1 - offsets)
    return jnp.stack([start, start + offsets], -1).astype(jnp.int32)


def draw_slot_count(key, part):
    key = jax.random.fold_in(key, 17)
    first, second, third = jax.random.split(key, 3)
    counts = jax.random.randint(first, (N_PAIR,), 1, P_DEV + 1)
    fullest = jax.random.randint(second, (), 0, N_PAIR)
    lightest = (fullest + 1 + jax.random.randint(third, (), 0, N_PAIR - 1)) % N_PAIR
    owners = jnp.arange(N_PAIR)
    counts = jnp.where(owners == lightest, 1, counts)
    return jnp.where(owners == fullest, P_DEV, counts).astype(jnp.int32)


def levels(key, extent, cuts, low, high):
    def one(dim, blocks):
        heights = jax.random.uniform(jax.random.fold_in(jax.random.fold_in(key, 6), dim), (blocks,), jnp.float32, low / len(cuts), high / len(cuts))
        return jnp.repeat(jnp.exp(heights), extent[dim] // blocks).reshape((-1,) + (1,) * (len(extent) - dim - 1))

    loudness = one(*cuts[0])
    for cut in cuts[1:]:
        loudness = loudness * one(*cut)
    return loudness


def bell_draw(stream_key, extent, scale, bound, cuts=(), kind=jnp.bfloat16):
    factor_of = levels(stream_key, extent, cuts, -0.22, 0.18) if cuts else 1.0
    values = jax.random.normal(stream_key, extent, jnp.float32) * scale * factor_of
    return jnp.minimum(jnp.maximum(values, -bound), bound).astype(kind)


def setup_inputs(seed: int = 0, part: int = 0) -> dict:
    keys = jax.random.split(jax.random.key(seed), 5)
    own_keys = jax.random.split(jax.random.fold_in(keys[4], part), 5)
    spectra = bell_draw(own_keys[0], (N_DAY_WIN, CHANNELS, SUBS, 2 * F), 1.0, 6.0, ((0, 4), (1, 4)))
    sub_pick = draw_sub_pick(jax.random.fold_in(keys[4], 71), part)
    pair_list = draw_pair_list(jax.random.fold_in(keys[4], 71), part)
    slot_count = draw_slot_count(jax.random.fold_in(keys[4], 71), part)
    return dict(spectra=spectra, sub_pick=sub_pick, pair_list=pair_list, slot_count=slot_count)


def lag_table(width, used):
    freq = jnp.arange(width, dtype=jnp.float32)[:, None]
    shift = (jnp.arange(LAGS) - LAGS // 2).astype(jnp.float32)[None, :]
    theta = jnp.pi * freq * shift / width
    scale = 1.0 / jnp.sqrt(jnp.float32(used * width))
    return jnp.concatenate([jnp.cos(theta) * scale, -jnp.sin(theta) * scale], 0).astype(jnp.bfloat16)

def reference(spectra, sub_pick, pair_list, slot_count):
    table = lag_table(F, SUB).astype(jnp.float32)
    index = sub_pick.astype(jnp.int32)[:, None, :, None]
    picked = jnp.take_along_axis(spectra, index, axis=2)
    blocks = picked.reshape(N_DAY_WIN, N_PAIR, CH_BLK, SUB, 2 * F)
    pairs = pair_list.reshape(SLOTS, 2)
    alive = (jnp.arange(P_DEV)[None, :] < slot_count[:, None]).reshape(SLOTS)

    def one(item):
        pair, live = item

        def add_day(day, total):
            left = blocks[day, pair[0]].astype(jnp.float32)
            right = blocks[day, pair[1]].astype(jnp.float32)
            lr, li = (left[..., :F], left[..., F:])
            rr, ri = (right[..., :F], right[..., F:])
            real = jnp.einsum('isf,jsf->ijf', lr, rr) + jnp.einsum('isf,jsf->ijf', li, ri)
            imag = jnp.einsum('isf,jsf->ijf', lr, ri) - jnp.einsum('isf,jsf->ijf', li, rr)
            cross = jnp.concatenate([real, imag], -1).astype(jnp.bfloat16)
            return total + cross.astype(jnp.float32)
        total = lax.fori_loop(0, N_DAY_WIN, add_day, jnp.zeros((CH_BLK, CH_BLK, 2 * F), jnp.float32))
        lagged = jnp.dot(total.reshape(CH_BLK * CH_BLK, 2 * F), table, precision=lax.Precision.HIGHEST, preferred_element_type=jnp.float32)
        lagged = lagged.reshape(CH_BLK, CH_BLK * LAGS)
        return jnp.where(live, lagged, jnp.zeros_like(lagged))
    return lax.map(one, (pairs, alive))
```

```python
import functools

import jax
import jax.numpy as jnp
import numpy as np
from jax import lax
from jax.experimental import pallas as pl
from jax.experimental.pallas import tpu as pltpu
from jax.sharding import PartitionSpec as P

LAGS = 64
HALF = LAGS // 2
REACH = 3
GROUP = 8
CHUNK = 256
MESH = pl.DeviceIdType.MESH


def lag_rows(width, used):
    freq = np.arange(width, dtype=np.float32)[None, :]
    shift = np.arange(HALF, dtype=np.float32)[:, None]
    shift_sin = shift.copy()
    shift_sin[0, 0] = -HALF
    scale = np.float32(1.0) / np.sqrt(np.float32(used * width))
    turn = np.float32(np.pi)
    cosine = np.cos(turn * freq * shift / np.float32(width)) * scale
    sine = -np.sin(turn * freq * shift_sin / np.float32(width)) * scale
    edge = np.zeros((16, width), np.float32)
    edge[0] = np.cos(turn * freq[0] * np.float32(-HALF) / np.float32(width)) * scale
    return jnp.asarray(np.concatenate([cosine, sine, edge], 0), jnp.bfloat16)


def lag_block(left_ref, right_ref, rows_ref, slot, row, width, used):
    chunks = width // CHUNK
    total = None
    piece = left_ref[slot, pl.ds(pl.multiple_of(row, GROUP), GROUP), :]
    for sub in range(used):
        for c in range(chunks):
            at = slice(c * CHUNK, (c + 1) * CHUNK)
            cos = rows_ref[0:HALF, at]
            sin_low = rows_ref[HALF : HALF + 16, at]
            sin_high = rows_ref[HALF + 16 : 2 * HALF, at]
            edge = rows_ref[2 * HALF : 2 * HALF + 16, at]
            start = sub * 2 * width + c * CHUNK
            real = piece[:, start : start + CHUNK]
            imag = piece[:, start + width : start + width + CHUNK]
            built = []
            for i in range(GROUP):
                re = jnp.broadcast_to(real[i : i + 1], (16, CHUNK)).astype(jnp.bfloat16)
                im = jnp.broadcast_to(imag[i : i + 1], (16, CHUNK)).astype(jnp.bfloat16)
                with_real = [
                    re * cos[:16], re * cos[16:], re * edge - im * sin_low, -(im * sin_high)
                ]
                with_imag = [
                    im * cos[:16], im * cos[16:], im * edge + re * sin_low, re * sin_high
                ]
                built.append(
                    jnp.concatenate(
                        [jnp.concatenate(with_real, 0), jnp.concatenate(with_imag, 0)], 1
                    )
                )
            weights = jnp.concatenate(built, 0)
            depth = (sub * chunks + c) * 2 * CHUNK
            part = jnp.dot(
                weights,
                right_ref[slot, depth : depth + 2 * CHUNK, :],
                preferred_element_type=jnp.float32,
            )
            total = part if total is None else total + part
    return total


def stack_kernel(
    days, width, used, left_ref, right_ref, rows_ref, out_ref, send, recv, send_sem, recv_sem
):
    slots, channels = left_ref.shape[0], left_ref.shape[1]
    share = channels // days
    steps = share // GROUP
    high = GROUP * LAGS
    me = lax.axis_index("day")

    barrier = pltpu.get_barrier_semaphore()
    for by in range(1, days):
        pl.semaphore_signal(
            barrier, inc=1, device_id={"day": lax.rem(me + by, days)}, device_id_type=MESH
        )

    def transfer(n):
        by = n // slots + 1
        return pltpu.make_async_remote_copy(
            src_ref=send.at[n],
            dst_ref=recv.at[n],
            send_sem=send_sem.at[n],
            recv_sem=recv_sem.at[n],
            device_id={"day": lax.rem(me + by, days)},
            device_id_type=MESH,
        )

    def block(slot, owner, step):
        return lag_block(
            left_ref, right_ref, rows_ref, slot, owner * share + step * GROUP, width, used
        )

    def send_piece(n, carry):
        owner = lax.rem(me + n // slots + 1, days)
        slot = lax.rem(n, slots)

        def one(step, inner):
            at = pl.ds(pl.multiple_of(step * high, high), high)
            send[n, at, :] = block(slot, owner, step).astype(jnp.bfloat16)
            return inner

        lax.fori_loop(0, steps, one, 0)

        @pl.when(n == 0)
        def _():
            pl.semaphore_wait(barrier, days - 1)

        transfer(n).start()
        return carry

    lax.fori_loop(0, (days - 1) * slots, send_piece, 0)

    def own_piece(n, carry):
        slot, step = n // steps, lax.rem(n, steps)
        at = pl.ds(pl.multiple_of(step * high, high), high)
        out_ref[slot, at, :] = block(slot, me, step)
        return carry

    lax.fori_loop(0, slots * steps, own_piece, 0)

    def add_piece(n, carry):
        slot = lax.rem(n, slots)
        transfer(n).wait()
        out_ref[slot] = out_ref[slot] + recv[n].astype(jnp.float32)
        return carry

    lax.fori_loop(0, (days - 1) * slots, add_piece, 0)


def stacked(left, right, rows, days, width, used):
    slots, channels = left.shape[0], left.shape[1]
    tall = channels // days * LAGS
    copies = (days - 1) * slots
    cost = 2 * slots * channels * LAGS * left.shape[2] * channels
    return pl.pallas_call(
        functools.partial(stack_kernel, days, width, used),
        out_shape=jax.ShapeDtypeStruct((slots, tall, channels), jnp.float32),
        in_specs=[pl.BlockSpec(memory_space=pltpu.VMEM)] * 3,
        out_specs=pl.BlockSpec(memory_space=pltpu.VMEM),
        scratch_shapes=[
            pltpu.VMEM((copies, tall, channels), jnp.bfloat16),
            pltpu.VMEM((copies, tall, channels), jnp.bfloat16),
            pltpu.SemaphoreType.DMA((copies,)),
            pltpu.SemaphoreType.DMA((copies,)),
        ],
        compiler_params=pltpu.CompilerParams(
            collective_id=0, has_side_effects=True, vmem_limit_bytes=48 * 1024 * 1024
        ),
        cost_estimate=pl.CostEstimate(flops=cost, bytes_accessed=1 << 23, transcendentals=0),
    )(left, right, rows)


def passed_along(value, by):
    count = lax.axis_size("pair")
    pairs = [(i, i + by) for i in range(count) if 0 <= i + by < count]
    return lax.ppermute(value, "pair", pairs)


def swapped(value, mask):
    count = lax.axis_size("pair")
    return lax.ppermute(value, "pair", [(i, i ^ mask) for i in range(count)])


def gathered(moved, wanted):
    here = lax.axis_index("pair")
    if lax.axis_size("pair") == 4:
        far = swapped(moved, 2)
        pool = jnp.stack([moved, swapped(moved, 1), far, swapped(far, 1)], 0)
        return pool, wanted ^ here
    nearby = [
        moved if step == 0 else passed_along(moved, -step) for step in range(-REACH, REACH + 1)
    ]
    return jnp.stack(nearby, 0), wanted - (here - REACH)


def per_device(spectra, sub_pick, pair_list, slot_count):
    local = spectra[0]
    picks = sub_pick[0]
    channels, width, used = local.shape[0], local.shape[2] // 2, picks.shape[0]
    days = lax.axis_size("day")
    moved = jnp.take(local, picks, axis=1).reshape(channels, used * 2 * width)
    pairs = pair_list[0]
    slots = pairs.shape[0]
    pool, place = gathered(moved, pairs)
    left = jnp.take(pool, place[:, 0], axis=0).astype(jnp.float32)
    right = jnp.take(pool, place[:, 1], axis=0)
    right = right.reshape(slots, channels, used, 2, width // CHUNK, CHUNK)
    right = right.transpose(0, 2, 4, 3, 5, 1).reshape(slots, used * 2 * width, channels)

    summed = stacked(left, right, lag_rows(width, used), days, width, used)
    summed = summed.reshape(slots, channels // days, LAGS, channels)
    even, odd = summed[:, :, :HALF], summed[:, :, HALF:]
    ahead = even[:, :, 1:] + odd[:, :, 1:]
    behind = even[:, :, 1:] - odd[:, :, 1:]
    lagged = jnp.concatenate([odd[:, :, :1], behind[:, :, ::-1], even[:, :, :1], ahead], 2)
    alive = (jnp.arange(slots) < slot_count[0])[:, None, None, None]
    lagged = jnp.where(alive, lagged, jnp.zeros_like(lagged))
    return lagged.transpose(0, 1, 3, 2).reshape(slots, channels // days, channels * LAGS)


def solution(mesh):
    in_specs = (
        P(("groups", "day"), "pair", None, None),
        P("day", None),
        P("pair", None, None),
        P("pair"),
    )
    out_specs = P(("groups", "pair"), "day", None)
    return jax.shard_map(
        per_device, mesh=mesh, in_specs=in_specs, out_specs=out_specs, check_vma=False
    )
```

```python
import functools

import jax
import jax.numpy as jnp
import numpy as np
from jax import lax
from jax.experimental import pallas as pl
from jax.experimental.pallas import tpu as pltpu
from jax.sharding import PartitionSpec as P

LAGS = 64
HALF = LAGS // 2
REACH = 3
GROUP = 8
CHUNK = 256
MESH = pl.DeviceIdType.MESH


def lag_rows(width, used):
    freq = np.arange(width, dtype=np.float32)[None, :]
    shift = np.arange(HALF, dtype=np.float32)[:, None]
    shift_sin = shift.copy()
    shift_sin[0, 0] = -HALF
    scale = np.float32(1.0) / np.sqrt(np.float32(used * width))
    turn = np.float32(np.pi)
    cosine = np.cos(turn * freq * shift / np.float32(width)) * scale
    sine = -np.sin(turn * freq * shift_sin / np.float32(width)) * scale
    edge = np.zeros((16, width), np.float32)
    edge[0] = np.cos(turn * freq[0] * np.float32(-HALF) / np.float32(width)) * scale
    return jnp.asarray(np.concatenate([cosine, sine, edge], 0), jnp.bfloat16)


def lag_block(left_ref, right_ref, rows_ref, slot, row, width, used):
    chunks = width // CHUNK
    total = None
    piece = left_ref[slot, pl.ds(pl.multiple_of(row, GROUP), GROUP), :]
    for sub in range(used):
        for c in range(chunks):
            at = slice(c * CHUNK, (c + 1) * CHUNK)
            cos = rows_ref[0:HALF, at]
            sin_low = rows_ref[HALF : HALF + 16, at]
            sin_high = rows_ref[HALF + 16 : 2 * HALF, at]
            edge = rows_ref[2 * HALF : 2 * HALF + 16, at]
            start = sub * 2 * width + c * CHUNK
            real = piece[:, start : start + CHUNK]
            imag = piece[:, start + width : start + width + CHUNK]
            built = []
            for i in range(GROUP):
                re = jnp.broadcast_to(real[i : i + 1], (16, CHUNK)).astype(jnp.bfloat16)
                im = jnp.broadcast_to(imag[i : i + 1], (16, CHUNK)).astype(jnp.bfloat16)
                with_real = [
                    re * cos[:16], re * cos[16:], re * edge - im * sin_low, -(im * sin_high)
                ]
                with_imag = [
                    im * cos[:16], im * cos[16:], im * edge + re * sin_low, re * sin_high
                ]
                built.append(
                    jnp.concatenate(
                        [jnp.concatenate(with_real, 0), jnp.concatenate(with_imag, 0)], 1
                    )
                )
            weights = jnp.concatenate(built, 0)
            depth = (sub * chunks + c) * 2 * CHUNK
            part = jnp.dot(
                weights,
                right_ref[slot, depth : depth + 2 * CHUNK, :],
                preferred_element_type=jnp.float32,
            )
            total = part if total is None else total + part
    return total


def laid_out(days, me):
    if days != 4:
        return lambda k: (lax.rem(me + k + 1, days), lax.rem(me + k + 1, days), k, k < 0)
    inner = lax.rem((me + 1) // 2, 2)
    low = 1 - me // 2

    def piece(k):
        outer_owner = low * (3 - k) + (1 - low) * k
        inner_first = low * 0 + (1 - low) * 3
        inner_owner = low * (4 - k) + (1 - low) * (k - 1)
        first = 1 - jnp.minimum(k, 1)
        inner_owner = first * inner_first + (1 - first) * inner_owner
        owner = inner * inner_owner + (1 - inner) * outer_owner
        target = inner * inner_owner + (1 - inner) * (low * 1 + (1 - low) * 2)
        landing = inner * (3 - first) + (1 - inner) * k
        return owner, target, landing, jnp.logical_and(inner == 1, k >= 1)

    return piece


def stack_kernel(
    days, width, used, left_ref, right_ref, rows_ref, out_ref,
    send, recv, own, fresh, turned, flat, send_sem, recv_sem,
):
    slots, channels = left_ref.shape[0], left_ref.shape[1]
    share = channels // days
    steps = share // GROUP
    high = GROUP * LAGS
    me = lax.axis_index("day")
    piece = laid_out(days, me)
    finals = (2, 3) if days == 4 else tuple(range(days - 1))

    barrier = pltpu.get_barrier_semaphore()
    for by in range(1, days):
        pl.semaphore_signal(
            barrier, inc=1, device_id={"day": lax.rem(me + by, days)}, device_id_type=MESH
        )

    def transfer(n, slot, target, landing):
        return pltpu.make_async_remote_copy(
            src_ref=send.at[n],
            dst_ref=recv.at[landing, slot],
            send_sem=send_sem.at[n],
            recv_sem=recv_sem.at[landing, slot],
            device_id={"day": target},
            device_id_type=MESH,
        )

    def span(step):
        return pl.ds(pl.multiple_of(step * high, high), high)

    def block(slot, owner, step):
        return lag_block(
            left_ref, right_ref, rows_ref, slot, owner * share + step * GROUP, width, used
        )

    def send_piece(n, carry):
        k, slot = n // slots, lax.rem(n, slots)
        owner, target, landing, adds = piece(k)

        def one(step, inner):
            fresh[span(step), :] = block(slot, owner, step)
            return inner

        lax.fori_loop(0, steps, one, 0)

        if days == 4:
            @pl.when(adds)
            def _():
                transfer(n, slot, target, k - 1).wait_recv()
                send[n] = (fresh[...] + recv[k - 1, slot].astype(jnp.float32)).astype(jnp.bfloat16)

            @pl.when(jnp.logical_not(adds))
            def _():
                send[n] = fresh[...].astype(jnp.bfloat16)
        else:
            send[n] = fresh[...].astype(jnp.bfloat16)

        @pl.when(n == 0)
        def _():
            pl.semaphore_wait(barrier, days - 1)

        transfer(n, slot, target, landing).start()
        return carry

    lax.fori_loop(0, (days - 1) * slots, send_piece, 0)

    def own_piece(n, carry):
        slot, step = n // steps, lax.rem(n, steps)
        own[slot, span(step), :] = block(slot, me, step)
        return carry

    lax.fori_loop(0, slots * steps, own_piece, 0)

    lane = lax.broadcasted_iota(jnp.int32, (LAGS, 2 * LAGS), 1)
    lag = lane % LAGS
    away = jnp.abs(lag - HALF)
    half = lane - lag
    even_at = half + away
    odd_at = half + HALF + jnp.minimum(away, HALF - 1)
    sign = jnp.where(lag > HALF, 1.0, jnp.where((lag > 0) & (lag < HALF), -1.0, 0.0))

    def joined(x):
        even = jnp.take_along_axis(x, even_at, axis=1)
        odd = jnp.take_along_axis(x, odd_at, axis=1)
        return even + sign * odd

    def finish(n, carry):
        slot, step = n // steps, lax.rem(n, steps)

        @pl.when(step == 0)
        def _():
            for f in finals:
                transfer(0, slot, lax.rem(me + 1, days), f).wait_recv()

        total = own[slot, span(step), :]
        for f in finals:
            total = total + recv[f, slot, span(step), :].astype(jnp.float32)
        for q in range(GROUP // 2):
            turned[q] = total[q * 2 * LAGS : (q + 1) * 2 * LAGS].T
        for q in range(GROUP // 2):
            first = turned[q, pl.ds(0, LAGS, stride=2), :]
            second = turned[q, pl.ds(1, LAGS, stride=2), :]
            flat[2 * q * LAGS : (2 * q + 1) * LAGS, :] = joined(
                jnp.where(lane < LAGS, first, pltpu.roll(second, LAGS, 1))
            )
            flat[(2 * q + 1) * LAGS : (2 * q + 2) * LAGS, :] = joined(
                jnp.where(lane < LAGS, pltpu.roll(first, LAGS, 1), second)
            )
        at = pl.ds(pl.multiple_of(step * GROUP, GROUP), GROUP)
        for m in range(channels // 2):
            out_ref[slot, at, m * 2 * LAGS : (m + 1) * 2 * LAGS] = flat[
                pl.ds(m, GROUP, stride=channels // 2), :
            ]
        return carry

    lax.fori_loop(0, slots * steps, finish, 0)

    def sent(n, carry):
        transfer(n, lax.rem(n, slots), lax.rem(me + 1, days), finals[0]).wait_send()
        return carry

    lax.fori_loop(0, (days - 1) * slots, sent, 0)


def stacked(left, right, rows, days, width, used):
    slots, channels = left.shape[0], left.shape[1]
    share = channels // days
    tall = share * LAGS
    copies = (days - 1) * slots
    landings = max(days - 1, 4)
    cost = 2 * slots * channels * LAGS * left.shape[2] * channels
    return pl.pallas_call(
        functools.partial(stack_kernel, days, width, used),
        out_shape=jax.ShapeDtypeStruct((slots, share, channels * LAGS), jnp.float32),
        in_specs=[pl.BlockSpec(memory_space=pltpu.VMEM)] * 3,
        out_specs=pl.BlockSpec(memory_space=pltpu.VMEM),
        scratch_shapes=[
            pltpu.VMEM((copies, tall, channels), jnp.bfloat16),
            pltpu.VMEM((landings, slots, tall, channels), jnp.bfloat16),
            pltpu.VMEM((slots, tall, channels), jnp.float32),
            pltpu.VMEM((tall, channels), jnp.float32),
            pltpu.VMEM((GROUP // 2, channels, 2 * LAGS), jnp.float32),
            pltpu.VMEM((GROUP * channels // 2, 2 * LAGS), jnp.float32),
            pltpu.SemaphoreType.DMA((copies,)),
            pltpu.SemaphoreType.DMA((landings, slots)),
        ],
        compiler_params=pltpu.CompilerParams(
            collective_id=0, has_side_effects=True, vmem_limit_bytes=48 * 1024 * 1024
        ),
        cost_estimate=pl.CostEstimate(flops=cost, bytes_accessed=1 << 23, transcendentals=0),
    )(left, right, rows)


def passed_along(value, by):
    count = lax.axis_size("pair")
    pairs = [(i, i + by) for i in range(count) if 0 <= i + by < count]
    return lax.ppermute(value, "pair", pairs)


def swapped(value, mask):
    count = lax.axis_size("pair")
    return lax.ppermute(value, "pair", [(i, i ^ mask) for i in range(count)])


def gathered(moved, wanted):
    here = lax.axis_index("pair")
    if lax.axis_size("pair") == 4:
        far = swapped(moved, 2)
        pool = jnp.stack([moved, swapped(moved, 1), far, swapped(far, 1)], 0)
        return pool, wanted ^ here
    nearby = [
        moved if step == 0 else passed_along(moved, -step) for step in range(-REACH, REACH + 1)
    ]
    return jnp.stack(nearby, 0), wanted - (here - REACH)


def per_device(spectra, sub_pick, pair_list, slot_count):
    local = spectra[0]
    picks = sub_pick[0]
    channels, width, used = local.shape[0], local.shape[2] // 2, picks.shape[0]
    days = lax.axis_size("day")
    moved = jnp.take(local, picks, axis=1).reshape(channels, used * 2 * width)
    pairs = pair_list[0]
    slots = pairs.shape[0]
    pool, place = gathered(moved, pairs)
    left = jnp.take(pool, place[:, 0], axis=0).astype(jnp.float32)
    right = jnp.take(pool, place[:, 1], axis=0)
    right = right.reshape(slots, channels, used, 2, width // CHUNK, CHUNK)
    right = right.transpose(0, 2, 4, 3, 5, 1).reshape(slots, used * 2 * width, channels)

    lagged = stacked(left, right, lag_rows(width, used), days, width, used)
    alive = (jnp.arange(slots) < slot_count[0])[:, None, None]
    return jnp.where(alive, lagged, jnp.zeros_like(lagged))


def solution(mesh):
    in_specs = (
        P(("groups", "day"), "pair", None, None),
        P("day", None),
        P("pair", None, None),
        P("pair"),
    )
    out_specs = P(("groups", "pair"), "day", None)
    return jax.shard_map(
        per_device, mesh=mesh, in_specs=in_specs, out_specs=out_specs, check_vma=False
    )
```

```python
import functools

import jax
import jax.numpy as jnp
import numpy as np
from jax import lax
from jax.experimental import pallas as pl
from jax.experimental.pallas import tpu as pltpu
from jax.sharding import PartitionSpec as P

LAGS = 64
HALF = LAGS // 2
REACH = 3
GROUP = 8
CHUNK = 256
MESH = pl.DeviceIdType.MESH


def lag_rows(width, used):
    freq = np.arange(width, dtype=np.float32)[None, :]
    shift = np.arange(HALF, dtype=np.float32)[:, None]
    shift_sin = shift.copy()
    shift_sin[0, 0] = -HALF
    scale = np.float32(1.0) / np.sqrt(np.float32(used * width))
    turn = np.float32(np.pi)
    cosine = np.cos(turn * freq * shift / np.float32(width)) * scale
    sine = -np.sin(turn * freq * shift_sin / np.float32(width)) * scale
    edge = np.zeros((16, width), np.float32)
    edge[0] = np.cos(turn * freq[0] * np.float32(-HALF) / np.float32(width)) * scale
    return jnp.asarray(np.concatenate([cosine, sine, edge], 0), jnp.bfloat16)


def lag_block(left_ref, right_ref, rows_ref, slot, row, width, used):
    chunks = width // CHUNK
    total = None
    piece = left_ref[slot, pl.ds(pl.multiple_of(row, GROUP), GROUP), :]
    for sub in range(used):
        for c in range(chunks):
            at = slice(c * CHUNK, (c + 1) * CHUNK)
            cos = rows_ref[0:HALF, at]
            sin_low = rows_ref[HALF : HALF + 16, at]
            sin_high = rows_ref[HALF + 16 : 2 * HALF, at]
            edge = rows_ref[2 * HALF : 2 * HALF + 16, at]
            start = sub * 2 * width + c * CHUNK
            real = piece[:, start : start + CHUNK]
            imag = piece[:, start + width : start + width + CHUNK]
            built = []
            for i in range(GROUP):
                re = jnp.broadcast_to(real[i : i + 1], (16, CHUNK)).astype(jnp.bfloat16)
                im = jnp.broadcast_to(imag[i : i + 1], (16, CHUNK)).astype(jnp.bfloat16)
                with_real = [
                    re * cos[:16], re * cos[16:], re * edge - im * sin_low, -(im * sin_high)
                ]
                with_imag = [
                    im * cos[:16], im * cos[16:], im * edge + re * sin_low, re * sin_high
                ]
                built.append(
                    jnp.concatenate(
                        [jnp.concatenate(with_real, 0), jnp.concatenate(with_imag, 0)], 1
                    )
                )
            weights = jnp.concatenate(built, 0)
            depth = (sub * chunks + c) * 2 * CHUNK
            part = jnp.dot(
                weights,
                right_ref[slot, depth : depth + 2 * CHUNK, :],
                preferred_element_type=jnp.float32,
            )
            total = part if total is None else total + part
    return total


def laid_out(days, me):
    if days != 4:
        return lambda k: (lax.rem(me + k + 1, days), lax.rem(me + k + 1, days), k, k < 0)
    inner = lax.rem((me + 1) // 2, 2)
    low = 1 - me // 2

    def piece(k):
        outer_owner = low * (3 - k) + (1 - low) * k
        inner_first = low * 0 + (1 - low) * 3
        inner_owner = low * (4 - k) + (1 - low) * (k - 1)
        first = 1 - jnp.minimum(k, 1)
        inner_owner = first * inner_first + (1 - first) * inner_owner
        owner = inner * inner_owner + (1 - inner) * outer_owner
        target = inner * inner_owner + (1 - inner) * (low * 1 + (1 - low) * 2)
        landing = inner * (3 - first) + (1 - inner) * k
        return owner, target, landing, jnp.logical_and(inner == 1, k >= 1)

    return piece


def fill_pool(near_ref, pool, ready, near_send, near_recv):
    here = lax.axis_index("pair")
    sibling, across = here + 1 - 2 * lax.rem(here, 2), lax.rem(here + 2, 4)
    tall = near_ref.shape[1] // 2

    def move(n, source, place, part, target):
        at = pl.ds(part * tall, tall)
        return pltpu.make_async_remote_copy(
            src_ref=source.at[at],
            dst_ref=pool.at[place, at],
            send_sem=near_send.at[n],
            recv_sem=near_recv.at[n],
            device_id={"pair": target},
            device_id_type=MESH,
        )

    far = [move(h, near_ref.at[0], 2, h, across) for h in range(2)]
    beside = [move(2 + h, near_ref.at[0], 1, h, sibling) for h in range(2)]
    passed = [move(4 + h, pool.at[2], 3, h, sibling) for h in range(2)]
    ready()
    for copy in far + beside:
        copy.start()
    pool[0] = near_ref[0]
    for h in range(2):
        far[h].wait_recv()
        passed[h].start()
    for copy in beside + passed:
        copy.wait_recv()
    return far + beside + passed


def stack_kernel(
    days, owners, width, used, near_ref, place_ref, rows_ref, out_ref,
    send, recv, own, fresh, turned, flat, left_ref, right_ref, pool, send_sem, recv_sem,
    near_send, near_recv,
):
    slots, channels = left_ref.shape[0], left_ref.shape[1]
    share = channels // days
    steps = share // GROUP
    high = GROUP * LAGS
    me = lax.axis_index("day")
    piece = laid_out(days, me)
    finals = (2, 3) if days == 4 else tuple(range(days - 1))

    barrier = pltpu.get_barrier_semaphore()
    for by in range(1, days):
        pl.semaphore_signal(
            barrier, inc=1, device_id={"day": lax.rem(me + by, days)}, device_id_type=MESH
        )
    moves = []
    if owners == 4:
        here = lax.axis_index("pair")
        for peer in (here + 1 - 2 * lax.rem(here, 2), lax.rem(here + 2, 4)):
            pl.semaphore_signal(barrier, inc=1, device_id={"pair": peer}, device_id_type=MESH)
        moves = fill_pool(
            near_ref, pool, lambda: pl.semaphore_wait(barrier, days + 1), near_send, near_recv
        )
        blocks = pool
    else:
        pl.semaphore_wait(barrier, days - 1)
        blocks = near_ref

    def unpack(slot, carry):
        a, b = place_ref[slot, 0], place_ref[slot, 1]
        for r in range(0, channels, 16):
            left_ref[slot, r : r + 16, :] = blocks[a, r : r + 16, :].astype(jnp.float32)
        parts = CHUNK // 128
        for sub in range(used):
            for e in range(2):
                for f in range(width // 128):
                    source = (sub * 2 + e) * width + f * 128
                    to = ((sub * (width // CHUNK) + f // parts) * 2 + e) * CHUNK + f % parts * 128
                    right_ref[slot, to : to + 128, :] = blocks[b, :, source : source + 128].T
        return carry

    lax.fori_loop(0, slots, unpack, 0)

    def transfer(n, slot, target, landing):
        return pltpu.make_async_remote_copy(
            src_ref=send.at[n],
            dst_ref=recv.at[landing, slot],
            send_sem=send_sem.at[n],
            recv_sem=recv_sem.at[landing, slot],
            device_id={"day": target},
            device_id_type=MESH,
        )

    def span(step):
        return pl.ds(pl.multiple_of(step * high, high), high)

    def block(slot, owner, step):
        return lag_block(
            left_ref, right_ref, rows_ref, slot, owner * share + step * GROUP, width, used
        )

    def send_piece(n, carry):
        k, slot = n // slots, lax.rem(n, slots)
        owner, target, landing, adds = piece(k)

        def one(step, inner):
            fresh[span(step), :] = block(slot, owner, step)
            return inner

        lax.fori_loop(0, steps, one, 0)

        if days == 4:
            @pl.when(adds)
            def _():
                transfer(n, slot, target, k - 1).wait_recv()
                send[n] = (fresh[...] + recv[k - 1, slot].astype(jnp.float32)).astype(jnp.bfloat16)

            @pl.when(jnp.logical_not(adds))
            def _():
                send[n] = fresh[...].astype(jnp.bfloat16)
        else:
            send[n] = fresh[...].astype(jnp.bfloat16)

        transfer(n, slot, target, landing).start()
        return carry

    lax.fori_loop(0, (days - 1) * slots, send_piece, 0)

    def own_piece(n, carry):
        slot, step = n // steps, lax.rem(n, steps)
        own[slot, span(step), :] = block(slot, me, step)
        return carry

    lax.fori_loop(0, slots * steps, own_piece, 0)

    lane = lax.broadcasted_iota(jnp.int32, (LAGS, 2 * LAGS), 1)
    lag = lane % LAGS
    away = jnp.abs(lag - HALF)
    half = lane - lag
    even_at = half + away
    odd_at = half + HALF + jnp.minimum(away, HALF - 1)
    sign = jnp.where(lag > HALF, 1.0, jnp.where((lag > 0) & (lag < HALF), -1.0, 0.0))

    def joined(x):
        even = jnp.take_along_axis(x, even_at, axis=1)
        odd = jnp.take_along_axis(x, odd_at, axis=1)
        return even + sign * odd

    def finish(n, carry):
        slot, step = n // steps, lax.rem(n, steps)

        @pl.when(step == 0)
        def _():
            for f in finals:
                transfer(0, slot, lax.rem(me + 1, days), f).wait_recv()

        total = own[slot, span(step), :]
        for f in finals:
            total = total + recv[f, slot, span(step), :].astype(jnp.float32)
        for q in range(GROUP // 2):
            turned[q] = total[q * 2 * LAGS : (q + 1) * 2 * LAGS].T
        for q in range(GROUP // 2):
            first = turned[q, pl.ds(0, LAGS, stride=2), :]
            second = turned[q, pl.ds(1, LAGS, stride=2), :]
            flat[2 * q * LAGS : (2 * q + 1) * LAGS, :] = joined(
                jnp.where(lane < LAGS, first, pltpu.roll(second, LAGS, 1))
            )
            flat[(2 * q + 1) * LAGS : (2 * q + 2) * LAGS, :] = joined(
                jnp.where(lane < LAGS, pltpu.roll(first, LAGS, 1), second)
            )
        at = pl.ds(pl.multiple_of(step * GROUP, GROUP), GROUP)
        for m in range(channels // 2):
            out_ref[slot, at, m * 2 * LAGS : (m + 1) * 2 * LAGS] = flat[
                pl.ds(m, GROUP, stride=channels // 2), :
            ]
        return carry

    lax.fori_loop(0, slots * steps, finish, 0)

    def sent(n, carry):
        transfer(n, lax.rem(n, slots), lax.rem(me + 1, days), finals[0]).wait_send()
        return carry

    lax.fori_loop(0, (days - 1) * slots, sent, 0)
    for copy in moves:
        copy.wait_send()


def stacked(near, place, rows, days, owners, width, used):
    slots, channels, depth = place.shape[0], near.shape[1], near.shape[2]
    share = channels // days
    tall = share * LAGS
    copies = (days - 1) * slots
    landings = max(days - 1, 4)
    cost = 2 * slots * channels * LAGS * depth * channels
    return pl.pallas_call(
        functools.partial(stack_kernel, days, owners, width, used),
        out_shape=jax.ShapeDtypeStruct((slots, share, channels * LAGS), jnp.float32),
        in_specs=[
            pl.BlockSpec(memory_space=pltpu.VMEM),
            pl.BlockSpec(memory_space=pltpu.SMEM),
            pl.BlockSpec(memory_space=pltpu.VMEM),
        ],
        out_specs=pl.BlockSpec(memory_space=pltpu.VMEM),
        scratch_shapes=[
            pltpu.VMEM((copies, tall, channels), jnp.bfloat16),
            pltpu.VMEM((landings, slots, tall, channels), jnp.bfloat16),
            pltpu.VMEM((slots, tall, channels), jnp.float32),
            pltpu.VMEM((tall, channels), jnp.float32),
            pltpu.VMEM((GROUP // 2, channels, 2 * LAGS), jnp.float32),
            pltpu.VMEM((GROUP * channels // 2, 2 * LAGS), jnp.float32),
            pltpu.VMEM((slots, channels, depth), jnp.float32),
            pltpu.VMEM((slots, depth, channels), jnp.bfloat16),
            pltpu.VMEM((4 if owners == 4 else 1, channels, depth), jnp.bfloat16),
            pltpu.SemaphoreType.DMA((copies,)),
            pltpu.SemaphoreType.DMA((landings, slots)),
            pltpu.SemaphoreType.DMA((6,)),
            pltpu.SemaphoreType.DMA((6,)),
        ],
        compiler_params=pltpu.CompilerParams(
            collective_id=0, has_side_effects=True, vmem_limit_bytes=48 * 1024 * 1024
        ),
        cost_estimate=pl.CostEstimate(flops=cost, bytes_accessed=1 << 23, transcendentals=0),
    )(near, place, rows)


def passed_along(value, by):
    count = lax.axis_size("pair")
    pairs = [(i, i + by) for i in range(count) if 0 <= i + by < count]
    return lax.ppermute(value, "pair", pairs)


def gathered(moved, wanted):
    here = lax.axis_index("pair")
    if lax.axis_size("pair") == 4:
        return moved[None], wanted ^ here
    nearby = [
        moved if step == 0 else passed_along(moved, -step) for step in range(-REACH, REACH + 1)
    ]
    return jnp.stack(nearby, 0), wanted - (here - REACH)


def per_device(spectra, sub_pick, pair_list, slot_count):
    local = spectra[0]
    picks = sub_pick[0]
    channels, width, used = local.shape[0], local.shape[2] // 2, picks.shape[0]
    days = lax.axis_size("day")
    moved = jnp.take(local, picks, axis=1).reshape(channels, used * 2 * width)
    pairs = pair_list[0]
    slots = pairs.shape[0]
    near, place = gathered(moved, pairs)
    owners = lax.axis_size("pair")
    lagged = stacked(near, place, lag_rows(width, used), days, owners, width, used)
    alive = (jnp.arange(slots) < slot_count[0])[:, None, None]
    return jnp.where(alive, lagged, jnp.zeros_like(lagged))


def solution(mesh):
    in_specs = (
        P(("groups", "day"), "pair", None, None),
        P("day", None),
        P("pair", None, None),
        P("pair"),
    )
    out_specs = P(("groups", "pair"), "day", None)
    return jax.shard_map(
        per_device, mesh=mesh, in_specs=in_specs, out_specs=out_specs, check_vma=False
    )
```

```python
import functools

import jax
import jax.numpy as jnp
import numpy as np
from jax import lax
from jax.experimental import pallas as pl
from jax.experimental.pallas import tpu as pltpu
from jax.sharding import PartitionSpec as P

LAGS = 64
HALF = LAGS // 2
REACH = 3
GROUP = 16
CHUNK = 256
MESH = pl.DeviceIdType.MESH


def lag_rows(width, used):
    freq = np.arange(width, dtype=np.float32)[None, :]
    shift = np.arange(HALF, dtype=np.float32)[:, None]
    shift_sin = shift.copy()
    shift_sin[0, 0] = -HALF
    scale = np.float32(1.0) / np.sqrt(np.float32(used * width))
    turn = np.float32(np.pi)
    cosine = np.cos(turn * freq * shift / np.float32(width)) * scale
    sine = -np.sin(turn * freq * shift_sin / np.float32(width)) * scale
    edge = np.zeros((16, width), np.float32)
    edge[0] = np.cos(turn * freq[0] * np.float32(-HALF) / np.float32(width)) * scale
    return jnp.asarray(np.concatenate([cosine, sine, edge], 0), jnp.bfloat16)


def lag_block(left_ref, right_ref, rows_ref, slot, row, width, used):
    chunks = width // CHUNK
    total = None
    piece = left_ref[slot, pl.ds(pl.multiple_of(row, GROUP), GROUP), :]
    for sub in range(used):
        for c in range(chunks):
            at = slice(c * CHUNK, (c + 1) * CHUNK)
            cos = rows_ref[0:HALF, at]
            sin_low = rows_ref[HALF : HALF + 16, at]
            sin_high = rows_ref[HALF + 16 : 2 * HALF, at]
            edge = rows_ref[2 * HALF : 2 * HALF + 16, at]
            start = sub * 2 * width + c * CHUNK
            real = piece[:, start : start + CHUNK]
            imag = piece[:, start + width : start + width + CHUNK]
            built = []
            for i in range(GROUP):
                re = jnp.broadcast_to(real[i : i + 1], (16, CHUNK)).astype(jnp.bfloat16)
                im = jnp.broadcast_to(imag[i : i + 1], (16, CHUNK)).astype(jnp.bfloat16)
                with_real = [
                    re * cos[:16], re * cos[16:], re * edge - im * sin_low, -(im * sin_high)
                ]
                with_imag = [
                    im * cos[:16], im * cos[16:], im * edge + re * sin_low, re * sin_high
                ]
                built.append(
                    jnp.concatenate(
                        [jnp.concatenate(with_real, 0), jnp.concatenate(with_imag, 0)], 1
                    )
                )
            weights = jnp.concatenate(built, 0)
            depth = (sub * chunks + c) * 2 * CHUNK
            part = jnp.dot(
                weights,
                right_ref[slot, depth : depth + 2 * CHUNK, :],
                preferred_element_type=jnp.float32,
            )
            total = part if total is None else total + part
    return total


def laid_out(days, me):
    if days != 4:
        return lambda k: (lax.rem(me + k + 1, days), lax.rem(me + k + 1, days), k, k < 0)
    inner = lax.rem((me + 1) // 2, 2)
    low = 1 - me // 2

    def piece(k):
        outer_owner = low * (3 - k) + (1 - low) * k
        inner_first = low * 0 + (1 - low) * 3
        inner_owner = low * (4 - k) + (1 - low) * (k - 1)
        first = 1 - jnp.minimum(k, 1)
        inner_owner = first * inner_first + (1 - first) * inner_owner
        owner = inner * inner_owner + (1 - inner) * outer_owner
        target = inner * inner_owner + (1 - inner) * (low * 1 + (1 - low) * 2)
        landing = inner * (3 - first) + (1 - inner) * k
        return owner, target, landing, jnp.logical_and(inner == 1, k >= 1)

    return piece


def fill_pool(near_ref, pool, ready, near_send, near_recv):
    here = lax.axis_index("pair")
    sibling, across = here + 1 - 2 * lax.rem(here, 2), lax.rem(here + 2, 4)
    tall = near_ref.shape[1] // 2

    def move(n, source, place, part, target):
        at = pl.ds(part * tall, tall)
        return pltpu.make_async_remote_copy(
            src_ref=source.at[at],
            dst_ref=pool.at[place, at],
            send_sem=near_send.at[n],
            recv_sem=near_recv.at[n],
            device_id={"pair": target},
            device_id_type=MESH,
        )

    far = [move(h, near_ref.at[0], 2, h, across) for h in range(2)]
    beside = [move(2 + h, near_ref.at[0], 1, h, sibling) for h in range(2)]
    passed = [move(4 + h, pool.at[2], 3, h, sibling) for h in range(2)]
    ready()
    for copy in far + beside:
        copy.start()
    pool[0] = near_ref[0]
    for h in range(2):
        far[h].wait_recv()
        passed[h].start()
    for copy in beside + passed:
        copy.wait_recv()
    return far + beside + passed


def helper_moves(near_ref, lent, me, lent_send, lent_recv):
    here = lax.axis_index("pair")
    sibling, across = here + 1 - 2 * lax.rem(here, 2), lax.rem(here + 2, 4)

    def move(n, source, place, device):
        return pltpu.make_async_remote_copy(
            src_ref=source,
            dst_ref=lent.at[place],
            send_sem=lent_send.at[n],
            recv_sem=lent_recv.at[n],
            device_id=device,
            device_id_type=MESH,
        )

    return [
        move(0, near_ref.at[0], 0, {"day": 1 + me // 2}),
        move(1, lent.at[0], 2, {"pair": across}),
        move(2, lent.at[0], 1, {"pair": sibling}),
        move(3, lent.at[2], 3, {"pair": sibling}),
    ]


def stack_kernel(
    days, owners, width, used, near_ref, place_ref, rows_ref, out_ref,
    send, recv, own, fresh, turned, flat, left_ref, right_ref, pool, send_sem, recv_sem,
    near_send, near_recv, lent, lent_send, lent_recv,
):
    helped = days == 4 and owners == 4
    slots, channels = left_ref.shape[0], left_ref.shape[1]
    share = channels // days
    steps = share // GROUP
    high = GROUP * LAGS
    me = lax.axis_index("day")
    piece = laid_out(days, me)
    finals = (2, 3) if days == 4 else tuple(range(days - 1))

    barrier = pltpu.get_barrier_semaphore()
    for by in range(1, days):
        pl.semaphore_signal(
            barrier, inc=1, device_id={"day": lax.rem(me + by, days)}, device_id_type=MESH
        )
    moves = []
    inner = lax.rem((me + 1) // 2, 2) == 1
    if helped:
        lend, lent_across, lent_beside, lent_passed = helper_moves(
            near_ref, lent, me, lent_send, lent_recv
        )

    def ready():
        pl.semaphore_wait(barrier, days + 1)
        if helped:
            @pl.when(jnp.logical_not(inner))
            def _():
                lend.start()

    if owners == 4:
        here = lax.axis_index("pair")
        for peer in (here + 1 - 2 * lax.rem(here, 2), lax.rem(here + 2, 4)):
            pl.semaphore_signal(barrier, inc=1, device_id={"pair": peer}, device_id_type=MESH)
        moves = fill_pool(near_ref, pool, ready, near_send, near_recv)
        blocks = pool
    else:
        pl.semaphore_wait(barrier, days - 1)
        blocks = near_ref

    if helped:
        @pl.when(inner)
        def _():
            lend.wait_recv()
            lent_across.start()
            lent_beside.start()

    def unpack(blocks, slot):
        a, b = place_ref[slot, 0], place_ref[slot, 1]
        for r in range(0, channels, 16):
            left_ref[slot, r : r + 16, :] = blocks[a, r : r + 16, :].astype(jnp.float32)
        parts = CHUNK // 128
        for sub in range(used):
            for e in range(2):
                for f in range(width // 128):
                    source = (sub * 2 + e) * width + f * 128
                    to = ((sub * (width // CHUNK) + f // parts) * 2 + e) * CHUNK + f % parts * 128
                    right_ref[slot, to : to + 128, :] = blocks[b, :, source : source + 128].T

    def unpack_own(slot, carry):
        unpack(blocks, slot)
        return carry

    lax.fori_loop(0, slots, unpack_own, 0)

    def transfer(n, slot, target, landing):
        return pltpu.make_async_remote_copy(
            src_ref=send.at[n],
            dst_ref=recv.at[landing, slot],
            send_sem=send_sem.at[n],
            recv_sem=recv_sem.at[landing, slot],
            device_id={"day": target},
            device_id_type=MESH,
        )

    def span(step):
        return pl.ds(pl.multiple_of(step * high, high), high)

    def block(slot, owner, step):
        return lag_block(
            left_ref, right_ref, rows_ref, slot, owner * share + step * GROUP, width, used
        )

    def send_piece(n):
        k, slot = n // slots, lax.rem(n, slots)
        owner, target, landing, adds = piece(k)

        def one(step, carry):
            fresh[span(step), :] = block(slot, owner, step)
            return carry

        lax.fori_loop(0, steps, one, 0)

        if days == 4:
            @pl.when(adds)
            def _():
                transfer(n, slot, target, k - 1).wait_recv()
                send[n] = (fresh[...] + recv[k - 1, slot].astype(jnp.float32)).astype(jnp.bfloat16)

            @pl.when(jnp.logical_not(adds))
            def _():
                send[n] = fresh[...].astype(jnp.bfloat16)
        else:
            send[n] = fresh[...].astype(jnp.bfloat16)

        transfer(n, slot, target, landing).start()

    def own_piece(n, carry):
        slot, step = n // steps, lax.rem(n, steps)
        own[slot, span(step), :] = block(slot, me, step)
        return carry

    def send_one(n, carry):
        send_piece(n)
        return carry

    copies = (days - 1) * slots
    last = slots - 1
    if helped:
        lax.fori_loop(0, copies - slots, send_one, 0)

        @pl.when(inner)
        def _():
            lent_across.wait_recv()
            lent_passed.start()

        lax.fori_loop(0, slots * steps, own_piece, 0)
        lax.fori_loop(copies - slots, copies - 1, send_one, 0)

        @pl.when(inner)
        def _():
            send_piece(copies - 1)
            lent_beside.wait_recv()
            lent_passed.wait_recv()
            unpack(lent, last)

            def extra(step, carry):
                recv[2, last, span(step), :] = block(last, me, step).astype(jnp.bfloat16)
                return carry

            lax.fori_loop(0, steps, extra, 0)
    else:
        lax.fori_loop(0, copies, send_one, 0)
        lax.fori_loop(0, slots * steps, own_piece, 0)

    lane = lax.broadcasted_iota(jnp.int32, (LAGS, 2 * LAGS), 1)
    lag = lane % LAGS
    away = jnp.abs(lag - HALF)
    half = lane - lag
    even_at = half + away
    odd_at = half + HALF + jnp.minimum(away, HALF - 1)
    sign = jnp.where(lag > HALF, 1.0, jnp.where((lag > 0) & (lag < HALF), -1.0, 0.0))

    def joined(x):
        even = jnp.take_along_axis(x, even_at, axis=1)
        odd = jnp.take_along_axis(x, odd_at, axis=1)
        return even + sign * odd

    def finish(n, carry):
        slot, step = n // steps, lax.rem(n, steps)

        for f in finals:
            landed = step == 0
            if helped and f == 2:
                landed = jnp.logical_and(
                    landed, jnp.logical_not(jnp.logical_and(inner, slot == last))
                )

            @pl.when(landed)
            def _():
                transfer(0, slot, lax.rem(me + 1, days), f).wait_recv()

        total = own[slot, span(step), :]
        for f in finals:
            total = total + recv[f, slot, span(step), :].astype(jnp.float32)
        for q in range(GROUP // 2):
            turned[q] = total[q * 2 * LAGS : (q + 1) * 2 * LAGS].T
        for q in range(GROUP // 2):
            first = turned[q, pl.ds(0, LAGS, stride=2), :]
            second = turned[q, pl.ds(1, LAGS, stride=2), :]
            flat[2 * q * LAGS : (2 * q + 1) * LAGS, :] = joined(
                jnp.where(lane < LAGS, first, pltpu.roll(second, LAGS, 1))
            )
            flat[(2 * q + 1) * LAGS : (2 * q + 2) * LAGS, :] = joined(
                jnp.where(lane < LAGS, pltpu.roll(first, LAGS, 1), second)
            )
        at = pl.ds(pl.multiple_of(step * GROUP, GROUP), GROUP)
        for m in range(channels // 2):
            out_ref[slot, at, m * 2 * LAGS : (m + 1) * 2 * LAGS] = flat[
                pl.ds(m, GROUP, stride=channels // 2), :
            ]
        return carry

    lax.fori_loop(0, slots * steps, finish, 0)

    def sent(n, carry):
        transfer(n, lax.rem(n, slots), lax.rem(me + 1, days), finals[0]).wait_send()
        return carry

    if helped:
        lax.fori_loop(0, copies - 1, sent, 0)

        @pl.when(inner)
        def _():
            sent(copies - 1, 0)
            lent_across.wait_send()
            lent_beside.wait_send()
            lent_passed.wait_send()

        @pl.when(jnp.logical_not(inner))
        def _():
            lend.wait_send()
    else:
        lax.fori_loop(0, copies, sent, 0)
    for copy in moves:
        copy.wait_send()


def stacked(near, place, rows, days, owners, width, used):
    slots, channels, depth = place.shape[0], near.shape[1], near.shape[2]
    share = channels // days
    tall = share * LAGS
    copies = (days - 1) * slots
    landings = max(days - 1, 4)
    cost = 2 * slots * channels * LAGS * depth * channels
    return pl.pallas_call(
        functools.partial(stack_kernel, days, owners, width, used),
        out_shape=jax.ShapeDtypeStruct((slots, share, channels * LAGS), jnp.float32),
        in_specs=[
            pl.BlockSpec(memory_space=pltpu.VMEM),
            pl.BlockSpec(memory_space=pltpu.SMEM),
            pl.BlockSpec(memory_space=pltpu.VMEM),
        ],
        out_specs=pl.BlockSpec(memory_space=pltpu.VMEM),
        scratch_shapes=[
            pltpu.VMEM((copies, tall, channels), jnp.bfloat16),
            pltpu.VMEM((landings, slots, tall, channels), jnp.bfloat16),
            pltpu.VMEM((slots, tall, channels), jnp.float32),
            pltpu.VMEM((tall, channels), jnp.float32),
            pltpu.VMEM((GROUP // 2, channels, 2 * LAGS), jnp.float32),
            pltpu.VMEM((GROUP * channels // 2, 2 * LAGS), jnp.float32),
            pltpu.VMEM((slots, channels, depth), jnp.float32),
            pltpu.VMEM((slots, depth, channels), jnp.bfloat16),
            pltpu.VMEM((4 if owners == 4 else 1, channels, depth), jnp.bfloat16),
            pltpu.SemaphoreType.DMA((copies,)),
            pltpu.SemaphoreType.DMA((landings, slots)),
            pltpu.SemaphoreType.DMA((6,)),
            pltpu.SemaphoreType.DMA((6,)),
            pltpu.VMEM((4 if owners == 4 else 1, channels, depth), jnp.bfloat16),
            pltpu.SemaphoreType.DMA((4,)),
            pltpu.SemaphoreType.DMA((4,)),
        ],
        compiler_params=pltpu.CompilerParams(
            collective_id=0, has_side_effects=True, vmem_limit_bytes=48 * 1024 * 1024
        ),
        cost_estimate=pl.CostEstimate(flops=cost, bytes_accessed=1 << 23, transcendentals=0),
    )(near, place, rows)


def passed_along(value, by):
    count = lax.axis_size("pair")
    pairs = [(i, i + by) for i in range(count) if 0 <= i + by < count]
    return lax.ppermute(value, "pair", pairs)


def gathered(moved, wanted):
    here = lax.axis_index("pair")
    if lax.axis_size("pair") == 4:
        return moved[None], wanted ^ here
    nearby = [
        moved if step == 0 else passed_along(moved, -step) for step in range(-REACH, REACH + 1)
    ]
    return jnp.stack(nearby, 0), wanted - (here - REACH)


def per_device(spectra, sub_pick, pair_list, slot_count):
    local = spectra[0]
    picks = sub_pick[0]
    channels, width, used = local.shape[0], local.shape[2] // 2, picks.shape[0]
    days = lax.axis_size("day")
    moved = jnp.take(local, picks, axis=1).reshape(channels, used * 2 * width)
    pairs = pair_list[0]
    slots = pairs.shape[0]
    near, place = gathered(moved, pairs)
    owners = lax.axis_size("pair")
    lagged = stacked(near, place, lag_rows(width, used), days, owners, width, used)
    alive = (jnp.arange(slots) < slot_count[0])[:, None, None]
    return jnp.where(alive, lagged, jnp.zeros_like(lagged))


def solution(mesh):
    in_specs = (
        P(("groups", "day"), "pair", None, None),
        P("day", None),
        P("pair", None, None),
        P("pair"),
    )
    out_specs = P(("groups", "pair"), "day", None)
    return jax.shard_map(
        per_device, mesh=mesh, in_specs=in_specs, out_specs=out_specs, check_vma=False
    )
```

```python
import functools

import jax
import jax.numpy as jnp
import numpy as np
from jax import lax
from jax.experimental import pallas as pl
from jax.experimental.pallas import tpu as pltpu
from jax.sharding import PartitionSpec as P

LAGS = 64
HALF = LAGS // 2
REACH = 3
GROUP = 16
CHUNK = 256
MESH = pl.DeviceIdType.MESH


def lag_rows(width, used):
    freq = np.arange(width, dtype=np.float32)[None, :]
    shift = np.arange(HALF, dtype=np.float32)[:, None]
    shift_sin = shift.copy()
    shift_sin[0, 0] = -HALF
    scale = np.float32(1.0) / np.sqrt(np.float32(used * width))
    turn = np.float32(np.pi)
    cosine = np.cos(turn * freq * shift / np.float32(width)) * scale
    sine = -np.sin(turn * freq * shift_sin / np.float32(width)) * scale
    edge = np.zeros((16, width), np.float32)
    edge[0] = np.cos(turn * freq[0] * np.float32(-HALF) / np.float32(width)) * scale
    return jnp.asarray(np.concatenate([cosine, sine, edge], 0), jnp.bfloat16)


def lag_block(left_ref, right_ref, rows_ref, slot, row, width, used):
    chunks = width // CHUNK
    total = None
    piece = left_ref[slot, pl.ds(pl.multiple_of(row, GROUP), GROUP), :]
    for sub in range(used):
        for c in range(chunks):
            at = slice(c * CHUNK, (c + 1) * CHUNK)
            cos = rows_ref[0:HALF, at]
            sin_low = rows_ref[HALF : HALF + 16, at]
            sin_high = rows_ref[HALF + 16 : 2 * HALF, at]
            edge = rows_ref[2 * HALF : 2 * HALF + 16, at]
            start = sub * 2 * width + c * CHUNK
            real = piece[:, start : start + CHUNK]
            imag = piece[:, start + width : start + width + CHUNK]
            built = []
            for i in range(GROUP):
                re = jnp.broadcast_to(real[i : i + 1], (16, CHUNK)).astype(jnp.bfloat16)
                im = jnp.broadcast_to(imag[i : i + 1], (16, CHUNK)).astype(jnp.bfloat16)
                with_real = [
                    re * cos[:16], re * cos[16:], re * edge - im * sin_low, -(im * sin_high)
                ]
                with_imag = [
                    im * cos[:16], im * cos[16:], im * edge + re * sin_low, re * sin_high
                ]
                built.append(
                    jnp.concatenate(
                        [jnp.concatenate(with_real, 0), jnp.concatenate(with_imag, 0)], 1
                    )
                )
            weights = jnp.concatenate(built, 0)
            depth = (sub * chunks + c) * 2 * CHUNK
            part = jnp.dot(
                weights,
                right_ref[slot, depth : depth + 2 * CHUNK, :],
                preferred_element_type=jnp.float32,
            )
            total = part if total is None else total + part
    return total


def laid_out(days, me):
    if days != 4:
        return lambda k: (lax.rem(me + k + 1, days), lax.rem(me + k + 1, days), k, k < 0)
    inner = lax.rem((me + 1) // 2, 2)
    low = 1 - me // 2

    def piece(k):
        outer_owner = low * (3 - k) + (1 - low) * k
        inner_first = low * 0 + (1 - low) * 3
        inner_owner = low * (4 - k) + (1 - low) * (k - 1)
        first = 1 - jnp.minimum(k, 1)
        inner_owner = first * inner_first + (1 - first) * inner_owner
        owner = inner * inner_owner + (1 - inner) * outer_owner
        target = inner * inner_owner + (1 - inner) * (low * 1 + (1 - low) * 2)
        landing = inner * (3 - first) + (1 - inner) * k
        return owner, target, landing, jnp.logical_and(inner == 1, k >= 1)

    return piece


def fill_pool(near_ref, pool, ready, near_send, near_recv):
    here = lax.axis_index("pair")
    sibling, across = here + 1 - 2 * lax.rem(here, 2), lax.rem(here + 2, 4)
    tall = near_ref.shape[1] // 2

    def move(n, source, place, part, target):
        at = pl.ds(part * tall, tall)
        return pltpu.make_async_remote_copy(
            src_ref=source.at[at],
            dst_ref=pool.at[place, at],
            send_sem=near_send.at[n],
            recv_sem=near_recv.at[n],
            device_id={"pair": target},
            device_id_type=MESH,
        )

    far = [move(h, near_ref.at[0], 2, h, across) for h in range(2)]
    beside = [move(2 + h, near_ref.at[0], 1, h, sibling) for h in range(2)]
    passed = [move(4 + h, pool.at[2], 3, h, sibling) for h in range(2)]
    ready()
    for copy in far + beside:
        copy.start()
    pool[0] = near_ref[0]
    for h in range(2):
        far[h].wait_recv()
        passed[h].start()
    for copy in beside + passed:
        copy.wait_recv()
    return far + beside + passed


def helper_moves(near_ref, lent, me, lent_send, lent_recv):
    here = lax.axis_index("pair")
    sibling, across = here + 1 - 2 * lax.rem(here, 2), lax.rem(here + 2, 4)

    def move(n, source, place, device):
        return pltpu.make_async_remote_copy(
            src_ref=source,
            dst_ref=lent.at[place],
            send_sem=lent_send.at[n],
            recv_sem=lent_recv.at[n],
            device_id=device,
            device_id_type=MESH,
        )

    return [
        move(0, near_ref.at[0], 0, {"day": 1 + me // 2}),
        move(1, lent.at[0], 2, {"pair": across}),
        move(2, lent.at[0], 1, {"pair": sibling}),
        move(3, lent.at[2], 3, {"pair": sibling}),
    ]


def stack_kernel(
    days, owners, width, used, near_ref, place_ref, rows_ref, out_ref,
    send, recv, own, fresh, turned, flat, left_ref, right_ref, pool, send_sem, recv_sem,
    near_send, near_recv, lent, lent_send, lent_recv,
):
    helped = days == 4 and owners == 4
    slots, channels = left_ref.shape[0], left_ref.shape[1]
    share = channels // days
    steps = share // GROUP
    high = GROUP * LAGS
    me = lax.axis_index("day")
    piece = laid_out(days, me)
    finals = (2, 3) if days == 4 else tuple(range(days - 1))

    barrier = pltpu.get_barrier_semaphore()
    for by in range(1, days):
        pl.semaphore_signal(
            barrier, inc=1, device_id={"day": lax.rem(me + by, days)}, device_id_type=MESH
        )
    moves = []
    inner = lax.rem((me + 1) // 2, 2) == 1
    if helped:
        lend, lent_across, lent_beside, lent_passed = helper_moves(
            near_ref, lent, me, lent_send, lent_recv
        )

    def ready():
        pl.semaphore_wait(barrier, days + 1)
        if helped:
            @pl.when(jnp.logical_not(inner))
            def _():
                lend.start()

    if owners == 4:
        here = lax.axis_index("pair")
        for peer in (here + 1 - 2 * lax.rem(here, 2), lax.rem(here + 2, 4)):
            pl.semaphore_signal(barrier, inc=1, device_id={"pair": peer}, device_id_type=MESH)
        moves = fill_pool(near_ref, pool, ready, near_send, near_recv)
        blocks = pool
    else:
        pl.semaphore_wait(barrier, days - 1)
        blocks = near_ref

    if helped:
        @pl.when(inner)
        def _():
            lend.wait_recv()
            lent_across.start()
            lent_beside.start()

    def unpack(blocks, slot):
        a, b = place_ref[slot, 0], place_ref[slot, 1]
        for r in range(0, channels, 16):
            left_ref[slot, r : r + 16, :] = blocks[a, r : r + 16, :].astype(jnp.float32)
        parts = CHUNK // 128
        for sub in range(used):
            for e in range(2):
                for f in range(width // 128):
                    source = (sub * 2 + e) * width + f * 128
                    to = ((sub * (width // CHUNK) + f // parts) * 2 + e) * CHUNK + f % parts * 128
                    right_ref[slot, to : to + 128, :] = blocks[b, :, source : source + 128].T

    def unpack_own(slot, carry):
        unpack(blocks, slot)
        return carry

    lax.fori_loop(0, slots, unpack_own, 0)

    def transfer(n, slot, target, landing):
        return pltpu.make_async_remote_copy(
            src_ref=send.at[n],
            dst_ref=recv.at[landing, slot],
            send_sem=send_sem.at[n],
            recv_sem=recv_sem.at[landing, slot],
            device_id={"day": target},
            device_id_type=MESH,
        )

    def span(step):
        return pl.ds(pl.multiple_of(step * high, high), high)

    def block(slot, owner, step):
        return lag_block(
            left_ref, right_ref, rows_ref, slot, owner * share + step * GROUP, width, used
        )

    copies = (days - 1) * slots
    last = slots - 1
    before = copies - slots if helped else copies
    jobs = before + slots + (slots + 1 if helped else 0)

    def job(n):
        is_own = jnp.logical_and(n >= before, n < before + slots)
        is_extra = n >= copies + slots
        at_home = jnp.logical_or(is_own, is_extra)
        sends = jnp.logical_not(at_home)
        out = jnp.where(n < before, n, jnp.minimum(jnp.maximum(n - slots, 0), copies - 1))
        k = out // slots
        slot = jnp.where(is_extra, last, lax.rem(n, slots))
        owner, target, landing, adds = piece(k)
        owner = jnp.where(at_home, me, owner)

        if helped:
            @pl.when(jnp.logical_and(inner, n == before))
            def _():
                lent_across.wait_recv()
                lent_passed.start()

            @pl.when(is_extra)
            def _():
                lent_beside.wait_recv()
                lent_passed.wait_recv()
                unpack(lent, last)

        def one(step, carry):
            fresh[span(step), :] = block(slot, owner, step)
            return carry

        lax.fori_loop(0, steps, one, 0)

        @pl.when(is_own)
        def _():
            own[slot] = fresh[...]

        if helped:
            @pl.when(is_extra)
            def _():
                recv[2, last] = fresh[...].astype(jnp.bfloat16)

        if days == 4:
            @pl.when(jnp.logical_and(sends, adds))
            def _():
                transfer(out, slot, target, k - 1).wait_recv()
                send[out] = (fresh[...] + recv[k - 1, slot].astype(jnp.float32)).astype(
                    jnp.bfloat16
                )

            @pl.when(jnp.logical_and(sends, jnp.logical_not(adds)))
            def _():
                send[out] = fresh[...].astype(jnp.bfloat16)
        else:
            @pl.when(sends)
            def _():
                send[out] = fresh[...].astype(jnp.bfloat16)

        @pl.when(sends)
        def _():
            transfer(out, slot, target, landing).start()

    def run(n, carry):
        if helped:
            pl.when(jnp.logical_or(inner, n < jobs - 2))(lambda: job(n))
        else:
            job(n)
        return carry

    lax.fori_loop(0, jobs, run, 0)

    lane = lax.broadcasted_iota(jnp.int32, (LAGS, 2 * LAGS), 1)
    lag = lane % LAGS
    order = lane - lag + jnp.where(lag < HALF, lax.rem(HALF - lag, HALF), lag)
    first_row = lax.broadcasted_iota(jnp.int32, (HALF, channels), 0) == 0

    def halves(x):
        even, odd = x[:HALF], x[HALF:]
        return [
            jnp.where(first_row, odd, even - odd), even + jnp.where(first_row, 0.0, odd)
        ]

    def joined(x):
        return jnp.take_along_axis(x, order, axis=1)

    def finish(n, carry):
        slot, step = n // steps, lax.rem(n, steps)

        for f in finals:
            landed = step == 0
            if helped and f == 2:
                landed = jnp.logical_and(
                    landed, jnp.logical_not(jnp.logical_and(inner, slot == last))
                )

            @pl.when(landed)
            def _():
                transfer(0, slot, lax.rem(me + 1, days), f).wait_recv()

        total = own[slot, span(step), :]
        for f in finals:
            total = total + recv[f, slot, span(step), :].astype(jnp.float32)
        for q in range(GROUP // 2):
            start = q * 2 * LAGS
            both = halves(total[start : start + LAGS])
            both += halves(total[start + LAGS : start + 2 * LAGS])
            turned[q] = jnp.concatenate(both, 0).T
        for q in range(GROUP // 2):
            first = turned[q, pl.ds(0, LAGS, stride=2), :]
            second = turned[q, pl.ds(1, LAGS, stride=2), :]
            flat[2 * q * LAGS : (2 * q + 1) * LAGS, :] = joined(
                jnp.where(lane < LAGS, first, pltpu.roll(second, LAGS, 1))
            )
            flat[(2 * q + 1) * LAGS : (2 * q + 2) * LAGS, :] = joined(
                jnp.where(lane < LAGS, pltpu.roll(first, LAGS, 1), second)
            )
        at = pl.ds(pl.multiple_of(step * GROUP, GROUP), GROUP)
        for m in range(channels // 2):
            out_ref[slot, at, m * 2 * LAGS : (m + 1) * 2 * LAGS] = flat[
                pl.ds(m, GROUP, stride=channels // 2), :
            ]
        return carry

    lax.fori_loop(0, slots * steps, finish, 0)

    def sent(n, carry):
        transfer(n, lax.rem(n, slots), lax.rem(me + 1, days), finals[0]).wait_send()
        return carry

    if helped:
        lax.fori_loop(0, copies - 1, sent, 0)

        @pl.when(inner)
        def _():
            sent(copies - 1, 0)
            lent_across.wait_send()
            lent_beside.wait_send()
            lent_passed.wait_send()

        @pl.when(jnp.logical_not(inner))
        def _():
            lend.wait_send()
    else:
        lax.fori_loop(0, copies, sent, 0)
    for copy in moves:
        copy.wait_send()


def stacked(near, place, rows, days, owners, width, used):
    slots, channels, depth = place.shape[0], near.shape[1], near.shape[2]
    share = channels // days
    tall = share * LAGS
    copies = (days - 1) * slots
    landings = max(days - 1, 4)
    cost = 2 * slots * channels * LAGS * depth * channels
    return pl.pallas_call(
        functools.partial(stack_kernel, days, owners, width, used),
        out_shape=jax.ShapeDtypeStruct((slots, share, channels * LAGS), jnp.float32),
        in_specs=[
            pl.BlockSpec(memory_space=pltpu.VMEM),
            pl.BlockSpec(memory_space=pltpu.SMEM),
            pl.BlockSpec(memory_space=pltpu.VMEM),
        ],
        out_specs=pl.BlockSpec(memory_space=pltpu.VMEM),
        scratch_shapes=[
            pltpu.VMEM((copies, tall, channels), jnp.bfloat16),
            pltpu.VMEM((landings, slots, tall, channels), jnp.bfloat16),
            pltpu.VMEM((slots, tall, channels), jnp.float32),
            pltpu.VMEM((tall, channels), jnp.float32),
            pltpu.VMEM((GROUP // 2, channels, 2 * LAGS), jnp.float32),
            pltpu.VMEM((GROUP * channels // 2, 2 * LAGS), jnp.float32),
            pltpu.VMEM((slots, channels, depth), jnp.float32),
            pltpu.VMEM((slots, depth, channels), jnp.bfloat16),
            pltpu.VMEM((4 if owners == 4 else 1, channels, depth), jnp.bfloat16),
            pltpu.SemaphoreType.DMA((copies,)),
            pltpu.SemaphoreType.DMA((landings, slots)),
            pltpu.SemaphoreType.DMA((6,)),
            pltpu.SemaphoreType.DMA((6,)),
            pltpu.VMEM((4 if owners == 4 else 1, channels, depth), jnp.bfloat16),
            pltpu.SemaphoreType.DMA((4,)),
            pltpu.SemaphoreType.DMA((4,)),
        ],
        compiler_params=pltpu.CompilerParams(
            collective_id=0, has_side_effects=True, vmem_limit_bytes=48 * 1024 * 1024
        ),
        cost_estimate=pl.CostEstimate(flops=cost, bytes_accessed=1 << 23, transcendentals=0),
    )(near, place, rows)


def passed_along(value, by):
    count = lax.axis_size("pair")
    pairs = [(i, i + by) for i in range(count) if 0 <= i + by < count]
    return lax.ppermute(value, "pair", pairs)


def gathered(moved, wanted):
    here = lax.axis_index("pair")
    if lax.axis_size("pair") == 4:
        return moved[None], wanted ^ here
    nearby = [
        moved if step == 0 else passed_along(moved, -step) for step in range(-REACH, REACH + 1)
    ]
    return jnp.stack(nearby, 0), wanted - (here - REACH)


def per_device(spectra, sub_pick, pair_list, slot_count):
    local = spectra[0]
    picks = sub_pick[0]
    channels, width, used = local.shape[0], local.shape[2] // 2, picks.shape[0]
    days = lax.axis_size("day")
    moved = jnp.take(local, picks, axis=1).reshape(channels, used * 2 * width)
    pairs = pair_list[0]
    slots = pairs.shape[0]
    near, place = gathered(moved, pairs)
    owners = lax.axis_size("pair")
    lagged = stacked(near, place, lag_rows(width, used), days, owners, width, used)
    alive = (jnp.arange(slots) < slot_count[0])[:, None, None]
    return jnp.where(alive, lagged, jnp.zeros_like(lagged))


def solution(mesh):
    in_specs = (
        P(("groups", "day"), "pair", None, None),
        P("day", None),
        P("pair", None, None),
        P("pair"),
    )
    out_specs = P(("groups", "pair"), "day", None)
    return jax.shard_map(
        per_device, mesh=mesh, in_specs=in_specs, out_specs=out_specs, check_vma=False
    )
```
